256 devices in a mesh: dp: 4 (over z_lo), ep: 64 (over x, y, z_hi, core).
Axes of the slice: x: 4, y: 4, z: 8 (z_hi: 2, z_lo: 4; z = z_hi * 4 + z_lo), core: 2. Of those that a mesh axis runs over, the one named last changes fastest.
Arguments:
- lengths: int32 [1536], P(('dp', 'ep')), may hold values from 0 to 62, as said below
- send_slots: int32 [256, 4, 1], P(('dp', 'ep')), may hold values from 0 to 6, as said below
- recv_slots: int32 [256, 4, 1], P(('dp', 'ep')), may hold values from 0 to 6, as said below
- latent_cache: bfloat16 [1536, 64, 576], P(('dp', 'ep')), may hold values from -5 to 5
- queries: bfloat16 [2, 1536, 64, 576], P(None, ('dp', 'ep')), may hold values from -24 to 24
- newest_kv: bfloat16 [2, 1536, 576], P(None, ('dp', 'ep')), may hold values from -5 to 5
- hidden_rows: bfloat16 [1536, 7168], P(('dp', 'ep')), may hold values from -6 to 6
- route_ids: int32 [2, 64, 24, 8], P(None, 'ep'), may hold values from 0 to 63, all different within a row; in each aligned block of 6 rows (0 to 5, 6 to 11, ..., all dimensions but the last counted through in order) at most 2 rows name the same one
- route_gates: int32 [2, 64, 24, 8], P(None, 'ep'), may hold values from 1 to 15
- w_gate: bfloat16 [64, 7168, 1024], P('ep', None, 'dp'), may hold values from -0.0625 to 0.0625
- w_up: bfloat16 [64, 7168, 1024], P('ep', None, 'dp'), may hold values from -0.0625 to 0.0625
- w_down: bfloat16 [64, 1024, 7168], P('ep', 'dp'), may hold values from -0.1875 to 0.1875
Outputs:
- attention: bfloat16 [2, 1536, 64, 512], P(None, ('dp', 'ep'))
- final_rows: bfloat16 [1536, 7168], P(('dp', 'ep'))
The draws below stay inside these ranges and needn't reach their ends.
Inputs may be any that keep to these rules, and one draw needn't show every extreme that they name: `lengths`: each index of ep has two ranks of dp with every slot live and two with one empty slot; live slots hold 1 to 62 positions, and 62 is reached in every index of ep. `send_slots`: in each index of ep the two full ranks each send one live request to one of the two other ranks, a different one each; at most 1 moves between two devices. `recv_slots`: entries describe the same moves as send_slots, entry m for entry m; a request lands in a slot empty before the move. `route_ids`: the 6 rows of one device name one expert at most 2 times.
All inputs are finite; a program needn't handle non-finite values.
Results may differ from the reference program's by a relative error of at most 0.018.
Values may be sent and summed in bfloat16 or wider, within the bound.
No kernel may reach another device: no remote copies, remote signals or barrier semaphores. Data moves between devices by JAX's collectives and lax.ppermute only.
A program may use at most 128 MiB of HBM per device.

```python
import math
import jax
import jax.numpy as jnp
import numpy as np
from jax import lax

D = 7168
LAT = 512
TOP = 8
FF = 1024
HEADS = 64
SLOTS = 6
CAP = 64
STEPS = 2
MIG = 1
KV = 576
DEV_CAP = 2
CAP_E = 8
SLOTS_ALL = 1536
N_DP = 4
N_EP = 64


def migration_plan(key):
    column_keys = jax.random.split(key, N_EP)

    def slot_order(one_key):
        return jax.random.permutation(one_key, SLOTS)

    def one_column(column_key):
        rank_key, slot_key, long_key, short_key = jax.random.split(column_key, 4)
        ranks = jax.random.permutation(rank_key, N_DP)
        roles = jnp.argsort(ranks)
        slot_orders = jax.vmap(slot_order)(jax.random.split(slot_key, N_DP))
        places = jnp.argsort(slot_orders, axis=1)
        heavy = roles < 2
        filled = jnp.where(heavy, SLOTS, SLOTS - 1)
        is_live = places < filled[:, None]
        long_len = jax.random.randint(long_key, (N_DP, SLOTS), CAP // 2, CAP - 1)
        short_len = jax.random.randint(short_key, (N_DP, SLOTS), 1, CAP // 2)
        sizes_now = jnp.where(is_live, jnp.where(heavy[:, None], long_len, short_len), 0)
        sizes_now = sizes_now.at[ranks[0], slot_orders[ranks[0], 0]].set(CAP - 2)
        sources = jnp.stack([ranks[0], ranks[1]])
        targets = jnp.stack([ranks[2], ranks[3]])
        outgoing = jnp.full((N_DP, N_DP), SLOTS, jnp.int32).at[sources, targets].set(slot_orders[sources, 0])
        incoming = jnp.full((N_DP, N_DP), SLOTS, jnp.int32).at[targets, sources].set(slot_orders[targets, SLOTS - 1])
        return (sizes_now.astype(jnp.int32), outgoing, incoming)
    sizes_all, outgoing_all, incoming_all = jax.vmap(one_column)(column_keys)
    lengths = jnp.transpose(sizes_all, (1, 0, 2)).reshape(N_DP * N_EP * SLOTS)
    sends = jnp.transpose(outgoing_all, (1, 0, 2)).reshape(N_DP * N_EP, N_DP, 1)
    receives = jnp.transpose(incoming_all, (1, 0, 2)).reshape(N_DP * N_EP, N_DP, 1)
    return (lengths, sends, receives)


def latent_rows(key):
    base = jax.random.normal(key, (SLOTS_ALL, CAP, KV), jnp.float32)
    return jnp.clip(base, -5.0, 5.0)


def draw_lengths(key, part):
    plan = migration_plan(key)
    return plan[0]


def draw_send_slots(key, part):
    plan = migration_plan(key)
    return plan[1]


def draw_recv_slots(key, part):
    plan = migration_plan(key)
    return plan[2]


def draw_latent_cache(key, part):
    stored = latent_rows(key)
    return stored.astype(jnp.bfloat16)


def draw_queries(key, part):
    key = jax.random.fold_in(key, 12)
    values = jnp.clip(jax.random.normal(key, (STEPS, SLOTS_ALL, HEADS, KV), jnp.float32), -5.0, 5.0)
    return values.astype(jnp.bfloat16)


def with_ends(array, key, smallest, top_value):
    place = [jax.random.randint(jax.random.fold_in(key, axis), (), 0, length) for axis, length in enumerate(array.shape)]
    longest = array.shape.index(max(array.shape))
    next_to = place[:longest] + [(place[longest] + 1) % array.shape[longest]] + place[longest + 1:]
    return array.at[tuple(place)].set(smallest).at[tuple(next_to)].set(top_value)


def levels(own_key, dims, cuts, least, largest):
    def one(position, parts):
        steps = jax.random.uniform(jax.random.fold_in(jax.random.fold_in(own_key, 6), position), (parts,), jnp.float32, least / len(cuts), largest / len(cuts))
        return jnp.repeat(jnp.exp(steps), dims[position] // parts).reshape((-1,) + (1,) * (len(dims) - position - 1))

    loudness = one(*cuts[0])
    for cut in cuts[1:]:
        loudness = loudness * one(*cut)
    return loudness


def shared_out(key, own, number, rows, number_of, top, reach, slope):
    sequence = jax.random.permutation(key, number_of)
    crowded, common = load_shares(number_of, rows * top, reach, slope, True), load_shares(number_of, rows * top, reach, slope, False)
    places = jnp.arange(number_of)

    def named(tallies, turn):
        used = int((tallies > 0).sum())
        fixed = max(1, used // 4)
        passed = fixed + (places - fixed + turn * (used - fixed)) % max(1, number_of - fixed)
        return jnp.zeros((number_of,), jnp.int32).at[sequence[jnp.where(places < fixed, places, passed)]].set(jnp.asarray(tallies, jnp.int32))

    tallies = jnp.where(number % 4 == 0, named(crowded, number // 4), named(common, number - number // 4 - 1))
    mixed = jax.random.permutation(jax.random.fold_in(own, 3), number_of)
    giver, receiver = mixed[0:number_of // 2 * 2:2], mixed[1:number_of // 2 * 2:2]
    room = jnp.minimum(tallies[giver] - 1, reach - tallies[receiver]) // 2
    room = jnp.where((giver == sequence[0]) | (receiver == sequence[0]) | (tallies[receiver] == 0), 0, jnp.maximum(room, 0))
    passed = jax.random.randint(jax.random.fold_in(own, 4), (number_of // 2,), 0, 1 << 20) % (room + 1)
    tallies = tallies.at[giver].add(-passed).at[receiver].add(passed)
    members = jnp.searchsorted(jnp.cumsum(tallies), jnp.arange(rows * top), side="right").astype(jnp.int32)
    table = members.reshape(top, rows).T
    table = table[jax.random.permutation(jax.random.fold_in(own, 1), rows)]
    turn = jax.random.randint(jax.random.fold_in(own, 2), (rows, 1), 0, top)
    return jnp.take_along_axis(table, (jnp.arange(top)[None, :] + turn) % top, axis=1)


def load_shares(number_of, total, reach, skew, full):
    weights = [(1 << 20) // math.isqrt(standing ** skew) + 1 for standing in range(1, number_of + 1)]
    largest = reach if full else min(reach, max(-(-total // number_of), total * weights[0] // sum(weights)))
    least = 1 if total - largest >= number_of - 1 else 0
    given, rest = [largest] + [least] * (number_of - 1), total - largest - least * (number_of - 1)
    while rest > 0:
        candidates = [i for i in range(1, number_of) if given[i] < largest] or [i for i in range(1, number_of) if given[i] < reach]
        pool, remaining = sum([weights[i] for i in candidates]), rest
        for i in candidates:
            extra = min(reach - given[i], max(1, remaining * weights[i] // pool), rest)
            given[i] = given[i] + extra
            rest = rest - extra
    return np.array(given)


def gaussian(key, dims, deviation, bound, cuts=(), kind=jnp.bfloat16):
    array = jax.random.normal(key, dims, jnp.float32) * deviation
    if len(cuts) > 0:
        array = levels(key, dims, cuts, -0.22, 0.18) * array
    return jnp.clip(array, min=-bound, max=bound).astype(kind)


def setup_inputs(seed: int = 0) -> dict:
    splits = jax.random.split(jax.random.key(seed), 13)
    lengths = draw_lengths(jax.random.fold_in(splits[12], 71), 0)
    send_slots = draw_send_slots(jax.random.fold_in(splits[12], 71), 0)
    recv_slots = draw_recv_slots(jax.random.fold_in(splits[12], 71), 0)
    latent_cache = draw_latent_cache(jax.random.fold_in(splits[12], 71), 0)
    queries = draw_queries(jax.random.fold_in(splits[12], 71), 0)
    newest_kv = gaussian(splits[5], (STEPS, SLOTS_ALL, KV), 1.0, 5.0, ((1, 256),))
    hidden_rows = gaussian(splits[6], (SLOTS_ALL, D), 1.0, 6.0, ((0, 256),))
    route_ids_keys = jax.random.split(jax.random.fold_in(splits[7], 1), STEPS * N_EP * (N_DP * SLOTS) // SLOTS)
    route_ids_turns = jax.random.permutation(jax.random.fold_in(splits[7], 3), STEPS * N_EP * (N_DP * SLOTS) // SLOTS)
    route_ids = jax.vmap(lambda own, number: shared_out(jax.random.fold_in(splits[7], 2), own, number, SLOTS, N_EP, TOP, DEV_CAP, 1))(route_ids_keys, route_ids_turns).reshape((STEPS, N_EP, N_DP * SLOTS, TOP))
    route_gates = with_ends(jax.random.randint(splits[8], (STEPS, N_EP, N_DP * SLOTS, TOP), 1, 16), jax.random.fold_in(splits[8], 1), 1, 15).astype(jnp.int32)
    w_gate = gaussian(splits[9], (N_EP, D, FF), D ** -0.5, 0.0625, ((0, 64), (2, 4)))
    w_up = gaussian(splits[10], (N_EP, D, FF), D ** -0.5, 0.0625, ((0, 64), (2, 4)))
    w_down = gaussian(splits[11], (N_EP, FF, D), FF ** -0.5, 0.1875, ((0, 64), (1, 4)))
    return dict(lengths=lengths, send_slots=send_slots, recv_slots=recv_slots, latent_cache=latent_cache, queries=queries, newest_kv=newest_kv, hidden_rows=hidden_rows, route_ids=route_ids, route_gates=route_gates, w_gate=w_gate, w_up=w_up, w_down=w_down)


softmax_scale = 192.0 ** (-0.5)
route_scale = 2.5
norm_eps = 1e-06

def normed_rows(hidden):
    values = hidden.astype(jnp.float32)
    inverse = lax.rsqrt(lax.optimization_barrier(jnp.mean(values * values, axis=1, keepdims=True)) + norm_eps)
    return (values * inverse).astype(jnp.bfloat16)

def decode_pass(cache_rows, queries_now, newest, counts):
    positions = lax.broadcasted_iota(jnp.int32, cache_rows.shape[:2], 1)
    is_live = counts > 0
    placed = (positions == counts[:, None]) & is_live[:, None]
    cache_rows = jnp.where(placed[:, :, None], newest[:, None, :], cache_rows)
    scores = jnp.einsum('nhk,ntk->nht', queries_now.astype(jnp.float32), cache_rows.astype(jnp.float32)) * softmax_scale
    usable = positions <= counts[:, None]
    scores = jnp.where(usable[:, None, :], scores, -1e+30)
    peak_score = lax.optimization_barrier(jnp.max(scores, axis=2, keepdims=True))
    raised = jnp.exp(scores - peak_score)
    chances = (raised / lax.optimization_barrier(jnp.sum(raised, axis=2, keepdims=True))).astype(jnp.bfloat16)
    output = jnp.einsum('nht,ntl->nhl', chances.astype(jnp.float32), cache_rows[:, :, :LAT].astype(jnp.float32))
    output = jnp.where(is_live[:, None, None], output, 0.0).astype(jnp.bfloat16)
    return (output, cache_rows)

def decode_all(cache_rows, queries_now, newest, counts):
    groups = N_DP * N_EP

    def one_group(bundle):
        return decode_pass(bundle[0], bundle[1], bundle[2], bundle[3])
    outputs, caches = lax.map(one_group, (cache_rows.reshape(groups, SLOTS, CAP, KV), queries_now.reshape(groups, SLOTS, HEADS, KV), newest.reshape(groups, SLOTS, KV), counts.reshape(groups, SLOTS)))
    return (outputs.reshape(SLOTS_ALL, HEADS, LAT), caches.reshape(SLOTS_ALL, CAP, KV))

def routed_layer(hidden, column_ids, column_gates, w_gate, w_up, w_down):
    fanout = column_ids.shape[2]
    token_count = hidden.shape[0]
    expert_ids = column_ids.reshape(N_EP, N_DP, SLOTS, fanout).transpose(1, 0, 2, 3).reshape(token_count * fanout)
    gate_float = column_gates.reshape(N_EP, N_DP, SLOTS, fanout).transpose(1, 0, 2, 3).reshape(token_count, fanout).astype(jnp.float32)
    weights = (route_scale * gate_float / lax.optimization_barrier(jnp.sum(gate_float, axis=1, keepdims=True))).reshape(-1)
    normed = normed_rows(hidden)
    route_count = token_count * fanout
    route_index = jnp.arange(route_count, dtype=jnp.int32)
    token_of = route_index // fanout
    ordering = jnp.argsort(expert_ids * route_count + route_index).astype(jnp.int32)
    expert_loads = lax.optimization_barrier(jnp.sum((expert_ids[:, None] == jnp.arange(N_EP, dtype=jnp.int32)[None, :]).astype(jnp.int32), axis=0))
    starts = jnp.cumsum(expert_loads) - expert_loads
    block_rows = min(64, N_EP * CAP_E)
    padded = jnp.concatenate([ordering, jnp.zeros((block_rows,), jnp.int32)])
    part_width = FF // N_DP

    def one_expert(summed_total, bundle):
        gate_matrix, up_matrix, down_matrix, expert_index = bundle
        block_count = (expert_loads[expert_index] + block_rows - 1) // block_rows

        def one_block(block_index, running):
            offset = starts[expert_index] + block_index * block_rows
            picked = lax.dynamic_slice_in_dim(padded, offset, block_rows)
            usable = block_index * block_rows + jnp.arange(block_rows, dtype=jnp.int32) < expert_loads[expert_index]
            gathered_rows = normed[token_of[picked]]
            gate_val = jnp.dot(gathered_rows, gate_matrix, preferred_element_type=jnp.float32)
            up_val = jnp.dot(gathered_rows, up_matrix, preferred_element_type=jnp.float32)
            inner_rows = (jax.nn.silu(gate_val) * up_val).astype(jnp.bfloat16)
            result = jnp.zeros((block_rows, hidden.shape[1]), jnp.float32)
            for part_index in range(N_DP):
                low_edge = part_index * part_width
                part_piece = jnp.dot(inner_rows[:, low_edge:low_edge + part_width], down_matrix[low_edge:low_edge + part_width], preferred_element_type=jnp.float32)
                result = result + lax.optimization_barrier(part_piece.astype(jnp.bfloat16)).astype(jnp.float32)
            factor = jnp.where(usable, weights[picked], 0.0)
            return running.at[token_of[picked]].add(result * factor[:, None])
        return (lax.fori_loop(0, block_count, one_block, summed_total), None)
    summed_total, unused = lax.scan(one_expert, jnp.zeros(hidden.shape, jnp.float32), (w_gate, w_up, w_down, jnp.arange(N_EP, dtype=jnp.int32)))
    return (hidden.astype(jnp.float32) + summed_total).astype(jnp.bfloat16)

def reference(lengths, send_slots, recv_slots, latent_cache, queries, newest_kv, hidden_rows, route_ids, route_gates, w_gate, w_up, w_down):
    first_att, cache_one = decode_all(latent_cache, queries[0], newest_kv[0], lengths)
    rows_one = routed_layer(hidden_rows, route_ids[0], route_gates[0], w_gate, w_up, w_down)
    counts_one = jnp.where(lengths > 0, lengths + 1, 0)
    outgoing = send_slots.reshape(N_DP, N_EP, N_DP, MIG)
    arriving = recv_slots.reshape(N_DP, N_EP, N_DP, MIG).transpose(2, 1, 0, 3)
    moving = outgoing < SLOTS
    grid_shape = outgoing.shape
    from_rank = lax.broadcasted_iota(jnp.int32, grid_shape, 0)
    column_index = lax.broadcasted_iota(jnp.int32, grid_shape, 1)
    to_rank = lax.broadcasted_iota(jnp.int32, grid_shape, 2)
    from_slot = (from_rank * N_EP + column_index) * SLOTS + outgoing
    to_slot = (to_rank * N_EP + column_index) * SLOTS + arriving
    slot_total = SLOTS_ALL
    source_of = jnp.arange(slot_total, dtype=jnp.int32).at[jnp.where(moving, to_slot, slot_total).reshape(-1)].set(from_slot.reshape(-1), mode='drop')
    vacated = jnp.zeros((slot_total,), jnp.int32).at[jnp.where(moving, from_slot, slot_total).reshape(-1)].set(1, mode='drop') > 0
    cache_two = cache_one[source_of]
    counts_two = jnp.where(vacated, 0, counts_one[source_of])
    rows_two = jnp.where(vacated[:, None], jnp.zeros_like(rows_one), rows_one[source_of])
    second_att, unused = decode_all(cache_two, queries[1], newest_kv[1], counts_two)
    final_rows = routed_layer(rows_two, route_ids[1], route_gates[1], w_gate, w_up, w_down)
    return (jnp.stack([first_att, second_att]), final_rows)
```

```python
import jax
import jax.numpy as jnp
from jax import lax
from jax.experimental import pallas as pl
from jax.experimental.pallas import tpu as pltpu
from jax.sharding import PartitionSpec as P

LAT = 512
WIDTH = 7168
GATE_COLS = 128
PAYLOAD = WIDTH + GATE_COLS
EXPERTS = 64
CHUNK = 1792
VMEM_LIMIT = 44 * 1024 * 1024
AXES = ("dp", "ep")
SIZES = {"x": 4, "y": 4, "z": 8}

softmax_scale = 192.0 ** (-0.5)
route_scale = 2.5
norm_eps = 1e-06


def device_index(x, y, z, core):
    return (z % 4) * 64 + ((x * 4 + y) * 2 + z // 4) * 2 + core


def every_device():
    return [
        (x, y, z, core)
        for x in range(SIZES["x"])
        for y in range(SIZES["y"])
        for z in range(SIZES["z"])
        for core in range(2)
    ]


def swap(value):
    pairs = [
        (device_index(x, y, z, core), device_index(x, y, z, 1 - core))
        for x, y, z, core in every_device()
    ]
    return lax.ppermute(value, AXES, pairs)


def shift(value, axis, distance):
    pairs = []
    for x, y, z, core in every_device():
        step = distance if core == 0 else -distance
        place = {"x": x, "y": y, "z": z}
        place[axis] = (place[axis] + step) % SIZES[axis]
        pairs.append(
            (device_index(x, y, z, core), device_index(place["x"], place["y"], place["z"], core))
        )
    return lax.ppermute(value, AXES, pairs)


def total(*values):
    result = values[0].astype(jnp.float32)
    for value in values[1:]:
        result = result + value.astype(jnp.float32)
    return result


def rounded(*values):
    return total(*values).astype(jnp.bfloat16)


def tied(values, others):
    held = lax.optimization_barrier((tuple(values), tuple(others)))
    return list(held[0]), list(held[1])


def expert_kernel(block_rows, steps, expert_ref, *refs):
    count = len(block_rows)
    rows_refs, route_refs = refs[:count], refs[count : 2 * count]
    gate_refs, up_refs, down_refs = (
        refs[2 * count : 2 * count + 2],
        refs[2 * count + 2 : 2 * count + 4],
        refs[2 * count + 4 : 2 * count + 6],
    )
    out_refs = refs[2 * count + 6 : 3 * count + 6]
    rows_all, gate_sum, up_sum, inner = refs[3 * count + 6 :]
    step = pl.program_id(0)

    @pl.when(step < steps)
    def _():
        start = 0
        for ref, size in zip(rows_refs, block_rows):
            rows_all[start : start + size, :] = ref[...]
            start += size
        rows_now = rows_all[...]
        gate_part = [
            jnp.dot(rows_now, ref[...], preferred_element_type=jnp.float32) for ref in gate_refs
        ]
        up_part = [
            jnp.dot(rows_now, ref[...], preferred_element_type=jnp.float32) for ref in up_refs
        ]

        @pl.when(step == 0)
        def _():
            for k in range(2):
                gate_sum[k] = gate_part[k]
                up_sum[k] = up_part[k]

        @pl.when(step > 0)
        def _():
            for k in range(2):
                gate_sum[k] += gate_part[k]
                up_sum[k] += up_part[k]

    @pl.when(step == steps - 1)
    def _():
        start = 0
        for ref, size in zip(route_refs, block_rows):
            routes = ref[...].astype(jnp.float32)
            column = lax.broadcasted_iota(jnp.int32, routes.shape, 1)
            whole = jnp.sum(jnp.where(column == EXPERTS, routes, 0.0), axis=1, keepdims=True)
            for k in range(2):
                mine = jnp.sum(
                    jnp.where(column == expert_ref[k], routes, 0.0), axis=1, keepdims=True
                )
                weight = route_scale * mine / whole
                gate_val = gate_sum[k, start : start + size, :]
                units = gate_val * jax.nn.sigmoid(gate_val) * up_sum[k, start : start + size, :]
                inner[k, start : start + size, :] = (units * weight).astype(jnp.bfloat16)
            start += size

    @pl.when(step >= steps)
    def _():
        result = jnp.dot(inner[0], down_refs[0][...], preferred_element_type=jnp.float32)
        result += jnp.dot(inner[1], down_refs[1][...], preferred_element_type=jnp.float32)
        result = result.astype(jnp.bfloat16)
        start = 0
        for ref, size in zip(out_refs, block_rows):
            ref[...] = result[start : start + size, :]
            start += size


def expert_call(blocks, expert, weights):
    block_rows = [block.shape[0] for block in blocks]
    rows = sum(block_rows)
    width = weights[0].shape[1]
    units = weights[0].shape[2]
    steps = width // CHUNK
    last = steps - 1

    def first_phase(k, expert_ref):
        return (0, jnp.minimum(k, last))

    def weight_in(k, expert_ref):
        return (0, jnp.minimum(k, last), 0)

    def weight_out(k, expert_ref):
        return (0, 0, jnp.maximum(k - steps, 0))

    def second_phase(k, expert_ref):
        return (0, jnp.maximum(k - steps, 0))

    def body(expert_ref, *refs):
        expert_kernel(block_rows, steps, expert_ref, *refs)

    return pl.pallas_call(
        body,
        grid_spec=pltpu.PrefetchScalarGridSpec(
            num_scalar_prefetch=1,
            grid=(2 * steps,),
            in_specs=[pl.BlockSpec((size, CHUNK), first_phase) for size in block_rows]
            + [
                pl.BlockSpec((size, GATE_COLS), lambda k, e: (0, WIDTH // GATE_COLS))
                for size in block_rows
            ]
            + [pl.BlockSpec((None, CHUNK, units), weight_in)] * 4
            + [pl.BlockSpec((None, units, CHUNK), weight_out)] * 2,
            out_specs=[pl.BlockSpec((size, CHUNK), second_phase) for size in block_rows],
            scratch_shapes=[
                pltpu.VMEM((rows, CHUNK), jnp.bfloat16),
                pltpu.VMEM((2, rows, units), jnp.float32),
                pltpu.VMEM((2, rows, units), jnp.float32),
                pltpu.VMEM((2, rows, units), jnp.bfloat16),
            ],
        ),
        out_shape=[jax.ShapeDtypeStruct((size, width), jnp.bfloat16) for size in block_rows],
        compiler_params=pltpu.CompilerParams(vmem_limit_bytes=VMEM_LIMIT),
        cost_estimate=pl.CostEstimate(
            flops=2 * rows * width * units * 6,
            bytes_accessed=6 * width * units * 2 + 2 * rows * width * 2,
            transcendentals=2 * rows * units,
        ),
    )(expert, *blocks, *blocks, *weights)


def normed_rows(hidden):
    values = hidden.astype(jnp.float32)
    inverse = lax.rsqrt(jnp.mean(values * values, axis=1, keepdims=True) + norm_eps)
    return (values * inverse).astype(jnp.bfloat16)


def decode_pass(cache_rows, queries_now, newest, counts):
    positions = lax.broadcasted_iota(jnp.int32, cache_rows.shape[:2], 1)
    is_live = counts > 0
    placed = (positions == counts[:, None]) & is_live[:, None]
    cache_rows = jnp.where(placed[:, :, None], newest[:, None, :], cache_rows)
    scores = (
        jnp.einsum("nhk,ntk->nht", queries_now, cache_rows, preferred_element_type=jnp.float32)
        * softmax_scale
    )
    usable = positions <= counts[:, None]
    scores = jnp.where(usable[:, None, :], scores, -1e30)
    peak_score = jnp.max(scores, axis=2, keepdims=True)
    raised = jnp.exp(scores - peak_score)
    chances = (raised / jnp.sum(raised, axis=2, keepdims=True)).astype(jnp.bfloat16)
    output = jnp.einsum(
        "nht,ntl->nhl", chances, cache_rows[:, :, :LAT], preferred_element_type=jnp.float32
    )
    output = jnp.where(is_live[:, None, None], output, 0.0).astype(jnp.bfloat16)
    return (output, cache_rows)


def route_columns(column_ids, column_gates, slot_count):
    first = lax.axis_index("dp") * slot_count
    ids = lax.dynamic_slice_in_dim(column_ids, first, slot_count, axis=0)
    gates = lax.dynamic_slice_in_dim(column_gates, first, slot_count, axis=0)
    column = lax.broadcasted_iota(jnp.int32, (1, 1, GATE_COLS), 2)
    spread = jnp.sum(jnp.where(ids[:, :, None] == column, gates[:, :, None], 0), axis=1)
    whole = jnp.sum(gates, axis=1, keepdims=True)
    column = lax.broadcasted_iota(jnp.int32, (1, GATE_COLS), 1)
    return jnp.where(column == EXPERTS, whole, spread).astype(jnp.bfloat16)


def send_direct(half, other, axis):
    reach = SIZES[axis] // 2
    both = jnp.concatenate([half, other], axis=0)
    return [shift(both, axis, k) for k in range(1, reach)] + [shift(half, axis, reach)]


def return_direct(sums, axis):
    reach = SIZES[axis] // 2
    rows = sums.shape[0] // SIZES[axis]
    arrived = [
        shift(sums[rows * (2 * k - 1) : rows * (2 * k + 1)], axis, -k) for k in range(1, reach)
    ]
    far = shift(sums[rows * (2 * reach - 1) :], axis, -reach)
    first = total(sums[:rows], far, *[piece[:rows] for piece in arrived])
    second = rounded(*[piece[rows:] for piece in arrived])
    return first, second


def routed_layer(hidden, routes, expert, weights):
    payload = jnp.concatenate([normed_rows(hidden), routes], axis=1)

    def experts(blocks):
        return expert_call(blocks, expert, weights)

    other = swap(payload)
    got = send_direct(payload[:4], other[:4], "z")
    got_z = send_direct(payload[4:], other[4:], "x")
    flat = jnp.concatenate([payload[4:], *got_z], axis=0)
    got_z = send_direct(flat, swap(flat), "y")
    z_half = jnp.concatenate([flat, *got_z], axis=0)
    column = jnp.concatenate([payload[:4], *got], axis=0)
    z_both = jnp.concatenate([z_half, swap(z_half)], axis=0)
    (z_both,), (column,) = tied([z_both], [column])
    z_near = shift(z_both, "z", 1)
    column = column.reshape(-1, 2, 2 * PAYLOAD)
    x_col = column[:, 0].reshape(-1, PAYLOAD)
    y_col = column[:, 1].reshape(-1, PAYLOAD)
    x_got = send_direct(x_col, swap(x_col), "y")
    y_got = send_direct(y_col, swap(y_col), "x")
    x_f = jnp.concatenate([x_col, *x_got], axis=0)
    y_f = jnp.concatenate([y_col, *y_got], axis=0)

    (x_f, y_f, z_near), _ = tied([x_f, y_f, z_near], [])
    x_g, y_g = swap(x_f), swap(y_f)
    x1f, y1f, z_mid = shift(x_f, "x", 1), shift(y_f, "y", 1), shift(z_near, "z", 1)
    first = experts([x_f, y_f, z_half, z_near])

    (x_g, y_g, z_mid), (x1f, y1f, *first) = tied([x_g, y_g, z_mid], [x1f, y1f, *first])
    x1g, y1g, z_far = shift(x_g, "x", 1), shift(y_g, "y", 1), shift(z_mid, "z", 1)
    second = experts([x1f, y1f, z_mid])

    (x1f_on, y1f_on, z_far), (x1g, y1g, *second) = tied([x1f, y1f, z_far], [x1g, y1g, *second])
    x2, y2 = shift(x1f_on, "x", 1), shift(y1f_on, "y", 1)
    z_end = shift(z_far[: z_far.shape[0] // 2], "z", 1)
    third = experts([x1g, y1g, z_far])
    (x2, y2, z_end), third = tied([x2, y2, z_end], third)
    last = experts([x2, y2, z_end])

    ox_f, oy_f, oz_half, tz_near = first
    tx1f, ty1f, tz_mid = second
    tx1g, ty1g, tz_far = third
    (tx2, ty2, tz_end), _ = tied(last, [])
    bx2, by2, bz_end = shift(tx2, "x", -1), shift(ty2, "y", -1), shift(tz_end, "z", -1)

    half = tz_end.shape[0]
    tx1f, ty1f = rounded(tx1f, bx2), rounded(ty1f, by2)
    tz_far = jnp.concatenate([rounded(tz_far[:half], bz_end), tz_far[half:]], axis=0)
    (tx1f, ty1f, tz_far), _ = tied([tx1f, ty1f, tz_far], [])
    bx1f, by1f, bz_far = shift(tx1f, "x", -1), shift(ty1f, "y", -1), shift(tz_far, "z", -1)

    tz_mid = rounded(tz_mid, bz_far)
    (tx1g, ty1g, tz_mid), (bx1f, by1f) = tied([tx1g, ty1g, tz_mid], [bx1f, by1f])
    bx1g, by1g, bz_mid = shift(tx1g, "x", -1), shift(ty1g, "y", -1), shift(tz_mid, "z", -1)

    tz_near = rounded(tz_near, bz_mid)
    (tz_near,), (bx1g, by1g) = tied([tz_near], [bx1g, by1g])
    bz_near = shift(tz_near, "z", -1)
    x_sum = rounded(ox_f, bx1f, swap(bx1g))
    y_sum = rounded(oy_f, by1f, swap(by1g))
    x_first, x_second = return_direct(x_sum, "y")
    y_first, y_second = return_direct(y_sum, "x")
    x_col = rounded(x_first, swap(x_second))
    y_col = rounded(y_first, swap(y_second))
    column = jnp.concatenate(
        [x_col.reshape(-1, 1, 2 * WIDTH), y_col.reshape(-1, 1, 2 * WIDTH)], axis=1
    ).reshape(-1, WIDTH)
    z_sum = rounded(oz_half, bz_near[:half], swap(bz_near[half:]))
    (column, z_sum), _ = tied([column, z_sum], [])
    first, second = return_direct(column, "z")
    z_first, z_second = return_direct(z_sum, "y")
    z_first, z_second = return_direct(rounded(z_first, swap(z_second)), "x")
    other = swap(jnp.concatenate([second, z_second], axis=0))
    addition = total(jnp.concatenate([first, z_first], axis=0), other)
    return (hidden.astype(jnp.float32) + addition).astype(jnp.bfloat16)


def from_peers(value):
    ranks = lax.axis_size("dp")
    return [
        lax.ppermute(value, "dp", [(i, (i + k) % ranks) for i in range(ranks)])
        for k in range(1, ranks)
    ]


def body(
    lengths,
    send_slots,
    recv_slots,
    latent_cache,
    queries,
    newest_kv,
    hidden_rows,
    route_ids,
    route_gates,
    w_gate,
    w_up,
    w_down,
):
    slot_count = lengths.shape[0]
    ranks = lax.axis_size("dp")
    rank = lax.axis_index("dp")
    expert = lax.axis_index("ep").astype(jnp.int32)
    expert = jnp.stack([expert, expert + 1 - 2 * (expert % 2)])
    local_slots = jnp.arange(slot_count, dtype=jnp.int32)
    leaving = jnp.min(send_slots)
    vacated = local_slots == leaving
    chosen = jnp.minimum(leaving, slot_count - 1)
    landings = [
        local_slots == lax.dynamic_index_in_dim(recv_slots[0, :, 0], (rank - k) % ranks, 0, False)
        for k in range(1, ranks)
    ]

    weights = [w_gate, swap(w_gate)]
    (later,), (weights[1],) = tied([w_up], [weights[1]])
    weights += [w_up, swap(later)]
    (later,), (weights[3],) = tied([w_down], [weights[3]])
    weights += [w_down, swap(later)]

    rows_one = routed_layer(
        hidden_rows,
        route_columns(route_ids[0, 0], route_gates[0, 0], slot_count),
        expert,
        weights,
    )

    first_att, cache_now = decode_pass(latent_cache, queries[0], newest_kv[0], lengths)
    counts_one = jnp.where(lengths > 0, lengths + 1, 0)
    cache_out = lax.dynamic_index_in_dim(cache_now, chosen, 0, False)
    count_out = lax.dynamic_index_in_dim(counts_one, chosen, 0, True).astype(jnp.bfloat16)
    moving = jnp.concatenate(
        [cache_out, jnp.broadcast_to(count_out, (8, cache_out.shape[1]))], axis=0
    )
    cap = cache_out.shape[0]
    cache_two = cache_now
    counts_two = jnp.where(vacated, 0, counts_one)
    for landing, arrived in zip(landings, from_peers(moving)):
        cache_two = jnp.where(landing[:, None, None], arrived[None, :cap], cache_two)
        counts_two = jnp.where(landing, arrived[cap, 0].astype(jnp.int32), counts_two)
    second_att, unused_cache = decode_pass(cache_two, queries[1], newest_kv[1], counts_two)

    row_out = lax.dynamic_index_in_dim(rows_one, chosen, 0, True)
    rows_two = jnp.where(vacated[:, None], jnp.zeros_like(rows_one), rows_one)
    for landing, row_in in zip(landings, from_peers(row_out)):
        rows_two = jnp.where(landing[:, None], row_in, rows_two)
    final_rows = routed_layer(
        rows_two,
        route_columns(route_ids[1, 0], route_gates[1, 0], slot_count),
        expert,
        weights,
    )
    return (jnp.stack([first_att, second_att]), final_rows)


def solution(mesh):
    return jax.shard_map(
        body,
        mesh=mesh,
        in_specs=(
            P(("dp", "ep")),
            P(("dp", "ep"), None, None),
            P(("dp", "ep"), None, None),
            P(("dp", "ep"), None, None),
            P(None, ("dp", "ep"), None, None),
            P(None, ("dp", "ep"), None),
            P(("dp", "ep"), None),
            P(None, "ep", None, None),
            P(None, "ep", None, None),
            P("ep", None, "dp"),
            P("ep", None, "dp"),
            P("ep", "dp", None),
        ),
        out_specs=(P(None, ("dp", "ep"), None, None), P(("dp", "ep"), None)),
        check_vma=False,
    )
```

```python
import jax
import jax.numpy as jnp
from jax import lax
from jax.experimental import pallas as pl
from jax.experimental.pallas import tpu as pltpu
from jax.sharding import PartitionSpec as P

LAT = 512
WIDTH = 7168
GATE_COLS = 128
PAYLOAD = WIDTH + GATE_COLS
EXPERTS = 64
CHUNK = 1024
AHEAD = 2
VMEM_LIMIT = 40 * 1024 * 1024
AXES = ("dp", "ep")
SIZES = {"x": 4, "y": 4, "z": 8}

softmax_scale = 192.0 ** (-0.5)
route_scale = 2.5
norm_eps = 1e-06


def device_index(x, y, z, core):
    return (z % 4) * 64 + ((x * 4 + y) * 2 + z // 4) * 2 + core


def every_device():
    return [
        (x, y, z, core)
        for x in range(SIZES["x"])
        for y in range(SIZES["y"])
        for z in range(SIZES["z"])
        for core in range(2)
    ]


def swap(value):
    pairs = [
        (device_index(x, y, z, core), device_index(x, y, z, 1 - core))
        for x, y, z, core in every_device()
    ]
    return lax.ppermute(value, AXES, pairs)


def shift(value, axis, distance, mirrored=True):
    pairs = []
    for x, y, z, core in every_device():
        step = -distance if core == 1 and mirrored else distance
        place = {"x": x, "y": y, "z": z}
        place[axis] = (place[axis] + step) % SIZES[axis]
        pairs.append(
            (device_index(x, y, z, core), device_index(place["x"], place["y"], place["z"], core))
        )
    return lax.ppermute(value, AXES, pairs)


def total(*values):
    result = values[0].astype(jnp.float32)
    for value in values[1:]:
        result = result + value.astype(jnp.float32)
    return result


def rounded(*values):
    return total(*values).astype(jnp.bfloat16)


def tied(values, others):
    held = lax.optimization_barrier((tuple(values), tuple(others)))
    return list(held[0]), list(held[1])


def together(*values):
    return lax.optimization_barrier(values)


def expert_kernel(block_rows, expert_ref, *refs):
    count = len(block_rows)
    rows_refs = refs[:count]
    weight_refs = refs[count : count + 6]
    out_refs = refs[count + 6 : 2 * count + 6]
    rows_all, inner, *held = refs[2 * count + 6 :]
    held, arrived = held[:6], held[6]
    copies = [
        pltpu.make_async_copy(source, target, arrived.at[k])
        for k, (source, target) in enumerate(zip(weight_refs, held))
    ]
    for copy in copies[:AHEAD]:
        copy.start()

    def arrive(k):
        copies[k].wait()
        if k + AHEAD < len(copies):
            copies[k + AHEAD].start()

    rows, width = rows_all.shape
    start = 0
    for ref, size in zip(rows_refs, block_rows):
        rows_all[start : start + size, :] = ref[:, :width]
        start += size
    routes = jnp.concatenate([ref[:, width:] for ref in rows_refs], axis=0).astype(jnp.float32)
    column = lax.broadcasted_iota(jnp.int32, routes.shape, 1)
    whole = jnp.sum(jnp.where(column == EXPERTS, routes, 0.0), axis=1, keepdims=True)
    for k in range(2):
        mine = jnp.sum(jnp.where(column == expert_ref[k], routes, 0.0), axis=1, keepdims=True)
        weight = route_scale * mine / whole
        arrive(2 * k)
        gate_val = jnp.dot(rows_all[...], held[2 * k][...], preferred_element_type=jnp.float32)
        arrive(2 * k + 1)
        up_val = jnp.dot(rows_all[...], held[2 * k + 1][...], preferred_element_type=jnp.float32)
        units = gate_val * jax.nn.sigmoid(gate_val) * up_val
        inner[k] = (units * weight).astype(jnp.bfloat16)
    arrive(4)
    arrive(5)

    @pl.loop(0, width // CHUNK)
    def _(step):
        columns = pl.ds(pl.multiple_of(step * CHUNK, CHUNK), CHUNK)
        result = jnp.dot(inner[0], held[4][:, columns], preferred_element_type=jnp.float32)
        result += jnp.dot(inner[1], held[5][:, columns], preferred_element_type=jnp.float32)
        result = result.astype(jnp.bfloat16)
        start = 0
        for ref, size in zip(out_refs, block_rows):
            ref[:, columns] = result[start : start + size, :]
            start += size


def expert_call(blocks, expert, weights):
    block_rows = [block.shape[0] for block in blocks]
    rows = sum(block_rows)
    width, units = weights[0].shape

    def body(expert_ref, *refs):
        expert_kernel(block_rows, expert_ref, *refs)

    whole = pl.BlockSpec(memory_space=pltpu.VMEM)
    return pl.pallas_call(
        body,
        in_specs=[pl.BlockSpec(memory_space=pltpu.SMEM)]
        + [whole] * len(blocks)
        + [pl.BlockSpec(memory_space=pl.ANY)] * len(weights),
        out_specs=[whole] * len(blocks),
        scratch_shapes=[
            pltpu.VMEM((rows, width), jnp.bfloat16),
            pltpu.VMEM((2, rows, units), jnp.bfloat16),
        ]
        + [pltpu.VMEM(weight.shape, jnp.bfloat16) for weight in weights]
        + [pltpu.SemaphoreType.DMA((len(weights),))],
        out_shape=[jax.ShapeDtypeStruct((size, width), jnp.bfloat16) for size in block_rows],
        compiler_params=pltpu.CompilerParams(vmem_limit_bytes=VMEM_LIMIT),
        cost_estimate=pl.CostEstimate(
            flops=2 * rows * width * units * 6,
            bytes_accessed=6 * width * units * 2 + 2 * rows * width * 2,
            transcendentals=2 * rows * units,
        ),
    )(expert, *blocks, *weights)


def normed_rows(hidden):
    values = hidden.astype(jnp.float32)
    inverse = lax.rsqrt(jnp.mean(values * values, axis=1, keepdims=True) + norm_eps)
    return (values * inverse).astype(jnp.bfloat16)


def decode_pass(cache_rows, queries_now, newest, counts):
    positions = lax.broadcasted_iota(jnp.int32, cache_rows.shape[:2], 1)
    is_live = counts > 0
    placed = (positions == counts[:, None]) & is_live[:, None]
    cache_rows = jnp.where(placed[:, :, None], newest[:, None, :], cache_rows)
    scores = (
        jnp.einsum("nhk,ntk->nht", queries_now, cache_rows, preferred_element_type=jnp.float32)
        * softmax_scale
    )
    usable = positions <= counts[:, None]
    scores = jnp.where(usable[:, None, :], scores, -1e30)
    peak_score = jnp.max(scores, axis=2, keepdims=True)
    raised = jnp.exp(scores - peak_score)
    chances = (raised / jnp.sum(raised, axis=2, keepdims=True)).astype(jnp.bfloat16)
    output = jnp.einsum(
        "nht,ntl->nhl", chances, cache_rows[:, :, :LAT], preferred_element_type=jnp.float32
    )
    output = jnp.where(is_live[:, None, None], output, 0.0).astype(jnp.bfloat16)
    return (output, cache_rows)


def route_columns(column_ids, column_gates, slot_count):
    first = lax.axis_index("dp") * slot_count
    ids = lax.dynamic_slice_in_dim(column_ids, first, slot_count, axis=0)
    gates = lax.dynamic_slice_in_dim(column_gates, first, slot_count, axis=0)
    column = lax.broadcasted_iota(jnp.int32, (1, 1, GATE_COLS), 2)
    spread = jnp.sum(jnp.where(ids[:, :, None] == column, gates[:, :, None], 0), axis=1)
    whole = jnp.sum(gates, axis=1, keepdims=True)
    column = lax.broadcasted_iota(jnp.int32, (1, GATE_COLS), 1)
    return jnp.where(column == EXPERTS, whole, spread).astype(jnp.bfloat16)


def routed_layer(hidden, routes, expert, weights):
    payload = jnp.concatenate([normed_rows(hidden), routes], axis=1)

    fetch = len(weights) == 3

    def experts(blocks):
        return expert_call(blocks, expert, weights)

    def fetched(place):
        return [swap(weights[place])] if fetch else []

    other = swap(payload)
    flat, half = payload[4:], payload[:4]
    both = jnp.concatenate([half, other[:4]], axis=0)
    z1, z2, near, far, *other_gate = together(
        shift(both, "z", 1),
        shift(both, "z", 2),
        shift(jnp.concatenate([flat, other[4:]], axis=0), "x", 1),
        shift(flat, "x", 2),
        *fetched(0),
    )
    flat = jnp.concatenate([flat, far, near], axis=0)
    x_col = jnp.concatenate([z1, z2], axis=0)
    z3, z4, ahead, behind, far, x_other = together(
        shift(both, "z", 3),
        shift(half, "z", 4),
        shift(flat, "y", 1, False),
        shift(flat, "y", -1, False),
        shift(flat, "y", 2, False),
        swap(x_col),
    )
    z_half = jnp.concatenate([flat, ahead, behind, far], axis=0)
    y_col = jnp.concatenate([z3, half, z4], axis=0)
    z_other, y_other = together(swap(z_half), swap(y_col))
    z_near, x_near, y_near, x_far, y_far, *other_rest = together(
        shift(jnp.concatenate([z_half, z_other], axis=0), "z", 1),
        shift(jnp.concatenate([x_col, x_other], axis=0), "y", 1),
        shift(jnp.concatenate([y_col, y_other], axis=0), "x", 1),
        shift(x_col, "y", 2),
        shift(y_col, "x", 2),
        *fetched(1),
        *fetched(2),
    )
    if fetch:
        w_gate, w_up, w_down = weights
        weights = [w_gate, w_up, *other_gate, other_rest[0], w_down, other_rest[1]]
    x_f = jnp.concatenate([x_col, x_far, x_near], axis=0)
    y_f = jnp.concatenate([y_col, y_far, y_near], axis=0)

    x1f, y1f, z_mid, x_g, y_g, *first = together(
        shift(x_f, "x", 1),
        shift(y_f, "y", 1),
        shift(z_near, "z", 1),
        swap(x_f),
        swap(y_f),
        *experts([x_f, y_f, z_half, z_near]),
    )
    x1g, y1g, z_far, x1f, y1f, z_mid, *second = together(
        shift(x_g, "x", 1),
        shift(y_g, "y", 1),
        shift(z_mid, "z", 1),
        x1f,
        y1f,
        z_mid,
        *experts([x1f, y1f, z_mid]),
    )
    x2, y2, z_end, *third = together(
        shift(x1f, "x", 1),
        shift(y1f, "y", 1),
        shift(z_far[: z_far.shape[0] // 2], "z", 1),
        *experts([x1g, y1g, z_far]),
    )

    ox_f, oy_f, oz_half, tz_near = first
    tx1f, ty1f, tz_mid = second
    tx1g, ty1g, tz_far = third
    bx1g, by1g, bz_far, tx2, ty2, tz_end = together(
        shift(tx1g, "x", -1),
        shift(ty1g, "y", -1),
        shift(tz_far, "z", -1),
        *experts([x2, y2, z_end]),
    )
    bz_end = shift(tz_end, "z", -4)
    bx2, by2, bz_mid = together(
        shift(tx2, "x", -1), shift(ty2, "y", -1), shift(rounded(tz_mid, bz_far), "z", -1)
    )
    size = tz_end.shape[0]
    bx1f, by1f, bz_near, bx1g, by1g = together(
        shift(rounded(tx1f, bx2), "x", -1),
        shift(rounded(ty1f, by2), "y", -1),
        shift(rounded(tz_near, bz_mid), "z", -1),
        swap(bx1g),
        swap(by1g),
    )
    x_sum = rounded(ox_f, bx1f, bx1g)
    y_sum = rounded(oy_f, by1f, by1g)
    n = x_sum.shape[0] // 4
    bz_end, x_near, y_near, x_far, y_far = together(
        bz_end,
        shift(x_sum[2 * n :], "y", -1),
        shift(y_sum[2 * n :], "x", -1),
        shift(x_sum[n : 2 * n], "y", -2),
        shift(y_sum[n : 2 * n], "x", -2),
    )
    x_other, y_other, z_other = together(swap(x_near[n:]), swap(y_near[n:]), swap(bz_near[size:]))
    x_col = rounded(x_sum[:n], x_far, x_near[:n], x_other)
    y_col = rounded(y_sum[:n], y_far, y_near[:n], y_other)
    z_sum = rounded(oz_half, bz_near[:size], bz_end, z_other)
    n = size // 4
    ahead, behind, far, z1, z2 = together(
        shift(z_sum[n : 2 * n], "y", -1, False),
        shift(z_sum[2 * n : 3 * n], "y", 1, False),
        shift(z_sum[3 * n :], "y", -2, False),
        shift(x_col[:8], "z", -1),
        shift(x_col[8:], "z", -2),
    )
    flat = rounded(z_sum[:n], ahead, behind, far)
    z3, z4, near, far = together(
        shift(y_col[:8], "z", -3),
        shift(y_col[12:], "z", -4),
        shift(flat[4:], "x", -1),
        shift(flat[2:4], "x", -2),
    )
    other = jnp.concatenate([rounded(z1[4:], z2[4:], z3[4:]), near[2:]], axis=0)
    mine = total(y_col[8:12], z1[:4], z2[:4], z3[:4], z4)
    mine = jnp.concatenate([mine, total(flat[:2], far, near[:2])], axis=0)
    result = hidden.astype(jnp.float32) + mine + swap(other).astype(jnp.float32)
    return result.astype(jnp.bfloat16), weights


def from_peers(value):
    ranks = lax.axis_size("dp")
    return [
        lax.ppermute(value, "dp", [(i, (i + k) % ranks) for i in range(ranks)])
        for k in range(1, ranks)
    ]


def body(
    lengths,
    send_slots,
    recv_slots,
    latent_cache,
    queries,
    newest_kv,
    hidden_rows,
    route_ids,
    route_gates,
    w_gate,
    w_up,
    w_down,
):
    slot_count = lengths.shape[0]
    ranks = lax.axis_size("dp")
    rank = lax.axis_index("dp")
    expert = lax.axis_index("ep").astype(jnp.int32)
    expert = jnp.stack([expert, expert + 1 - 2 * (expert % 2)])
    local_slots = jnp.arange(slot_count, dtype=jnp.int32)
    leaving = jnp.min(send_slots)
    vacated = local_slots == leaving
    chosen = jnp.minimum(leaving, slot_count - 1)
    landings = [
        local_slots == lax.dynamic_index_in_dim(recv_slots[0, :, 0], (rank - k) % ranks, 0, False)
        for k in range(1, ranks)
    ]

    rows_one, weights = routed_layer(
        hidden_rows,
        route_columns(route_ids[0, 0], route_gates[0, 0], slot_count),
        expert,
        [w_gate[0], w_up[0], w_down[0]],
    )

    first_att, cache_now = decode_pass(latent_cache, queries[0], newest_kv[0], lengths)
    counts_one = jnp.where(lengths > 0, lengths + 1, 0)
    cache_out = lax.dynamic_index_in_dim(cache_now, chosen, 0, False)
    count_out = lax.dynamic_index_in_dim(counts_one, chosen, 0, True).astype(jnp.bfloat16)
    moving = jnp.concatenate(
        [cache_out, jnp.broadcast_to(count_out, (8, cache_out.shape[1]))], axis=0
    )
    cap = cache_out.shape[0]
    cache_two = cache_now
    counts_two = jnp.where(vacated, 0, counts_one)
    for landing, arrived in zip(landings, from_peers(moving)):
        cache_two = jnp.where(landing[:, None, None], arrived[None, :cap], cache_two)
        counts_two = jnp.where(landing, arrived[cap, 0].astype(jnp.int32), counts_two)
    second_att, unused_cache = decode_pass(cache_two, queries[1], newest_kv[1], counts_two)

    row_out = lax.dynamic_index_in_dim(rows_one, chosen, 0, True)
    rows_two = jnp.where(vacated[:, None], jnp.zeros_like(rows_one), rows_one)
    for landing, row_in in zip(landings, from_peers(row_out)):
        rows_two = jnp.where(landing[:, None], row_in, rows_two)
    final_rows, weights = routed_layer(
        rows_two,
        route_columns(route_ids[1, 0], route_gates[1, 0], slot_count),
        expert,
        weights,
    )
    return (jnp.stack([first_att, second_att]), final_rows)


def solution(mesh):
    return jax.shard_map(
        body,
        mesh=mesh,
        in_specs=(
            P(("dp", "ep")),
            P(("dp", "ep"), None, None),
            P(("dp", "ep"), None, None),
            P(("dp", "ep"), None, None),
            P(None, ("dp", "ep"), None, None),
            P(None, ("dp", "ep"), None),
            P(("dp", "ep"), None),
            P(None, "ep", None, None),
            P(None, "ep", None, None),
            P("ep", None, "dp"),
            P("ep", None, "dp"),
            P("ep", "dp", None),
        ),
        out_specs=(P(None, ("dp", "ep"), None, None), P(("dp", "ep"), None)),
        check_vma=False,
    )
```

```python
import jax
import jax.numpy as jnp
from jax import lax
from jax.experimental import pallas as pl
from jax.experimental.pallas import tpu as pltpu
from jax.sharding import PartitionSpec as P

LAT = 512
WIDTH = 7168
GATE_COLS = 128
PAYLOAD = WIDTH + GATE_COLS
EXPERTS = 64
CHUNK = 1024
VMEM_LIMIT = 26 * 1024 * 1024
AXES = ("dp", "ep")
SIZES = {"x": 4, "y": 4, "z": 8}

softmax_scale = 192.0 ** (-0.5)
route_scale = 2.5
norm_eps = 1e-06


def device_index(x, y, z, core):
    return (z % 4) * 64 + ((x * 4 + y) * 2 + z // 4) * 2 + core


def every_device():
    return [
        (x, y, z, core)
        for x in range(SIZES["x"])
        for y in range(SIZES["y"])
        for z in range(SIZES["z"])
        for core in range(2)
    ]


def swap(value):
    pairs = [
        (device_index(x, y, z, core), device_index(x, y, z, 1 - core))
        for x, y, z, core in every_device()
    ]
    return lax.ppermute(value, AXES, pairs)


def shift(value, axis, distance, mirrored=True):
    pairs = []
    for x, y, z, core in every_device():
        step = -distance if core == 1 and mirrored else distance
        place = {"x": x, "y": y, "z": z}
        place[axis] = (place[axis] + step) % SIZES[axis]
        pairs.append(
            (device_index(x, y, z, core), device_index(place["x"], place["y"], place["z"], core))
        )
    return lax.ppermute(value, AXES, pairs)


def total(*values):
    result = values[0].astype(jnp.float32)
    for value in values[1:]:
        result = result + value.astype(jnp.float32)
    return result


def rounded(*values):
    return total(*values).astype(jnp.bfloat16)


def tied(values, others):
    held = lax.optimization_barrier((tuple(values), tuple(others)))
    return list(held[0]), list(held[1])


def together(*values):
    return lax.optimization_barrier(values)


def expert_kernel(block_rows, expert_ref, *refs):
    count = len(block_rows)
    rows_refs = refs[:count]
    weight_refs = refs[count : count + 6]
    out_refs = refs[count + 6 : 2 * count + 6]
    rows_all, inner, *held = refs[2 * count + 6 :]
    arrived = held[4]
    held = [held[0], held[1], held[0], held[1], held[2], held[3]]
    copies = [
        pltpu.make_async_copy(source, target, arrived.at[k])
        for k, (source, target) in enumerate(zip(weight_refs, held))
    ]
    copies[0].start()
    copies[1].start()

    rows, width = rows_all.shape
    start = 0
    for ref, size in zip(rows_refs, block_rows):
        rows_all[start : start + size, :] = ref[:, :width]
        start += size
    routes = jnp.concatenate([ref[:, width:] for ref in rows_refs], axis=0).astype(jnp.float32)
    column = lax.broadcasted_iota(jnp.int32, routes.shape, 1)
    whole = jnp.sum(jnp.where(column == EXPERTS, routes, 0.0), axis=1, keepdims=True)
    for k in range(2):
        mine = jnp.sum(jnp.where(column == expert_ref[k], routes, 0.0), axis=1, keepdims=True)
        weight = route_scale * mine / whole
        copies[2 * k].wait()
        gate_val = jnp.dot(rows_all[...], held[2 * k][...], preferred_element_type=jnp.float32)
        copies[2 * k + 2].start()
        copies[2 * k + 1].wait()
        up_val = jnp.dot(rows_all[...], held[2 * k + 1][...], preferred_element_type=jnp.float32)
        copies[2 * k + 3].start()
        units = gate_val * jax.nn.sigmoid(gate_val) * up_val
        inner[k] = (units * weight).astype(jnp.bfloat16)
    copies[4].wait()
    copies[5].wait()

    @pl.loop(0, width // CHUNK)
    def _(step):
        columns = pl.ds(pl.multiple_of(step * CHUNK, CHUNK), CHUNK)
        result = jnp.dot(inner[0], held[4][:, columns], preferred_element_type=jnp.float32)
        result += jnp.dot(inner[1], held[5][:, columns], preferred_element_type=jnp.float32)
        result = result.astype(jnp.bfloat16)
        start = 0
        for ref, size in zip(out_refs, block_rows):
            ref[:, columns] = result[start : start + size, :]
            start += size


def expert_call(blocks, expert, weights):
    block_rows = [block.shape[0] for block in blocks]
    rows = sum(block_rows)
    width, units = weights[0].shape

    def body(expert_ref, *refs):
        expert_kernel(block_rows, expert_ref, *refs)

    whole = pl.BlockSpec(memory_space=pltpu.VMEM)
    return pl.pallas_call(
        body,
        in_specs=[pl.BlockSpec(memory_space=pltpu.SMEM)]
        + [whole] * len(blocks)
        + [pl.BlockSpec(memory_space=pl.ANY)] * len(weights),
        out_specs=[whole] * len(blocks),
        scratch_shapes=[
            pltpu.VMEM((rows, width), jnp.bfloat16),
            pltpu.VMEM((2, rows, units), jnp.bfloat16),
        ]
        + [pltpu.VMEM(weight.shape, jnp.bfloat16) for weight in weights[2:]]
        + [pltpu.SemaphoreType.DMA((len(weights),))],
        out_shape=[jax.ShapeDtypeStruct((size, width), jnp.bfloat16) for size in block_rows],
        compiler_params=pltpu.CompilerParams(vmem_limit_bytes=VMEM_LIMIT),
        cost_estimate=pl.CostEstimate(
            flops=2 * rows * width * units * 6,
            bytes_accessed=6 * width * units * 2 + 2 * rows * width * 2,
            transcendentals=2 * rows * units,
        ),
    )(expert, *blocks, *weights)


def normed_rows(hidden):
    values = hidden.astype(jnp.float32)
    inverse = lax.rsqrt(jnp.mean(values * values, axis=1, keepdims=True) + norm_eps)
    return (values * inverse).astype(jnp.bfloat16)


def decode_pass(cache_rows, queries_now, newest, counts):
    positions = lax.broadcasted_iota(jnp.int32, cache_rows.shape[:2], 1)
    is_live = counts > 0
    placed = (positions == counts[:, None]) & is_live[:, None]
    cache_rows = jnp.where(placed[:, :, None], newest[:, None, :], cache_rows)
    scores = (
        jnp.einsum("nhk,ntk->nht", queries_now, cache_rows, preferred_element_type=jnp.float32)
        * softmax_scale
    )
    usable = positions <= counts[:, None]
    scores = jnp.where(usable[:, None, :], scores, -1e30)
    peak_score = jnp.max(scores, axis=2, keepdims=True)
    raised = jnp.exp(scores - peak_score)
    chances = (raised / jnp.sum(raised, axis=2, keepdims=True)).astype(jnp.bfloat16)
    output = jnp.einsum(
        "nht,ntl->nhl", chances, cache_rows[:, :, :LAT], preferred_element_type=jnp.float32
    )
    output = jnp.where(is_live[:, None, None], output, 0.0).astype(jnp.bfloat16)
    return (output, cache_rows)


def route_columns(column_ids, column_gates, slot_count):
    first = lax.axis_index("dp") * slot_count
    ids = lax.dynamic_slice_in_dim(column_ids, first, slot_count, axis=0)
    gates = lax.dynamic_slice_in_dim(column_gates, first, slot_count, axis=0)
    column = lax.broadcasted_iota(jnp.int32, (1, 1, GATE_COLS), 2)
    spread = jnp.sum(jnp.where(ids[:, :, None] == column, gates[:, :, None], 0), axis=1)
    whole = jnp.sum(gates, axis=1, keepdims=True)
    column = lax.broadcasted_iota(jnp.int32, (1, GATE_COLS), 1)
    return jnp.where(column == EXPERTS, whole, spread).astype(jnp.bfloat16)


def routed_layer(hidden, routes, expert, weights):
    payload = jnp.concatenate([normed_rows(hidden), routes], axis=1)

    fetch = len(weights) == 3

    def experts(blocks):
        return expert_call(blocks, expert, weights)

    def fetched(place):
        return [swap(weights[place])] if fetch else []

    other, *other_gate = together(swap(payload), *fetched(0))
    flat, half = payload[4:], payload[:4]
    both = jnp.concatenate([half, other[:4]], axis=0)
    z1, z2, near, far, *other_up = together(
        shift(both, "z", 1),
        shift(both, "z", 2),
        shift(jnp.concatenate([flat, other[4:]], axis=0), "x", 1),
        shift(flat, "x", 2),
        *fetched(1),
    )
    flat = jnp.concatenate([flat, far, near], axis=0)
    x_col = jnp.concatenate([z1, z2], axis=0)
    z3, z4, ahead, behind, far, x_other = together(
        shift(both, "z", 3),
        shift(half, "z", 4),
        shift(flat, "y", 1, False),
        shift(flat, "y", -1, False),
        shift(flat, "y", 2, False),
        swap(x_col),
    )
    z_half = jnp.concatenate([flat, ahead, behind, far], axis=0)
    y_col = jnp.concatenate([z3, half, z4], axis=0)
    z_other, y_other, *down_now = together(
        swap(z_half), swap(y_col), *(weights[2:] if fetch else [])
    )
    z_near, x_near, y_near, x_far, y_far, *other_down = together(
        shift(jnp.concatenate([z_half, z_other], axis=0), "z", 1),
        shift(jnp.concatenate([x_col, x_other], axis=0), "y", 1),
        shift(jnp.concatenate([y_col, y_other], axis=0), "x", 1),
        shift(x_col, "y", 2),
        shift(y_col, "x", 2),
        *([swap(down_now[0])] if fetch else []),
    )
    if fetch:
        w_gate, w_up, w_down = weights
        weights = [w_gate, w_up, *other_gate, *other_up, w_down, *other_down]
    x_f = jnp.concatenate([x_col, x_far, x_near], axis=0)
    y_f = jnp.concatenate([y_col, y_far, y_near], axis=0)

    x1f, y1f, z_mid, x_g, y_g, *first = together(
        shift(x_f, "x", 1),
        shift(y_f, "y", 1),
        shift(z_near, "z", 1),
        swap(x_f),
        swap(y_f),
        *experts([x_f, y_f, z_half, z_near]),
    )
    x1g, y1g, z_far, x1f, y1f, z_mid, *second = together(
        shift(x_g, "x", 1),
        shift(y_g, "y", 1),
        shift(z_mid, "z", 1),
        x1f,
        y1f,
        z_mid,
        *experts([x1f, y1f, z_mid]),
    )
    x2, y2, z_end, *third = together(
        shift(x1f, "x", 1),
        shift(y1f, "y", 1),
        shift(z_far[: z_far.shape[0] // 2], "z", 1),
        *experts([x1g, y1g, z_far]),
    )

    ox_f, oy_f, oz_half, tz_near = first
    tx1f, ty1f, tz_mid = second
    tx1g, ty1g, tz_far = third
    bx1g, by1g, bz_far, tx2, ty2, tz_end = together(
        shift(tx1g, "x", -1),
        shift(ty1g, "y", -1),
        shift(tz_far, "z", -1),
        *experts([x2, y2, z_end]),
    )
    bz_end = shift(tz_end, "z", -4)
    bx2, by2, bz_mid = together(
        shift(tx2, "x", -1), shift(ty2, "y", -1), shift(rounded(tz_mid, bz_far), "z", -1)
    )
    size = tz_end.shape[0]
    bx1f, by1f, bz_near, bx1g, by1g = together(
        shift(rounded(tx1f, bx2), "x", -1),
        shift(rounded(ty1f, by2), "y", -1),
        shift(rounded(tz_near, bz_mid), "z", -1),
        swap(bx1g),
        swap(by1g),
    )
    x_sum = rounded(ox_f, bx1f, bx1g)
    y_sum = rounded(oy_f, by1f, by1g)
    n = x_sum.shape[0] // 4
    bz_end, x_near, y_near, x_far, y_far = together(
        bz_end,
        shift(x_sum[2 * n :], "y", -1),
        shift(y_sum[2 * n :], "x", -1),
        shift(x_sum[n : 2 * n], "y", -2),
        shift(y_sum[n : 2 * n], "x", -2),
    )
    x_other, y_other, z_other = together(swap(x_near[n:]), swap(y_near[n:]), swap(bz_near[size:]))
    x_col = rounded(x_sum[:n], x_far, x_near[:n], x_other)
    y_col = rounded(y_sum[:n], y_far, y_near[:n], y_other)
    z_sum = rounded(oz_half, bz_near[:size], bz_end, z_other)
    n = size // 4
    ahead, behind, far, z1, z2 = together(
        shift(z_sum[n : 2 * n], "y", -1, False),
        shift(z_sum[2 * n : 3 * n], "y", 1, False),
        shift(z_sum[3 * n :], "y", -2, False),
        shift(x_col[:8], "z", -1),
        shift(x_col[8:], "z", -2),
    )
    flat = rounded(z_sum[:n], ahead, behind, far)
    z3, z4, near, far = together(
        shift(y_col[:8], "z", -3),
        shift(y_col[12:], "z", -4),
        shift(flat[4:], "x", -1),
        shift(flat[2:4], "x", -2),
    )
    other = jnp.concatenate([rounded(z1[4:], z2[4:], z3[4:]), near[2:]], axis=0)
    mine = total(y_col[8:12], z1[:4], z2[:4], z3[:4], z4)
    mine = jnp.concatenate([mine, total(flat[:2], far, near[:2])], axis=0)
    result = hidden.astype(jnp.float32) + mine + swap(other).astype(jnp.float32)
    return result.astype(jnp.bfloat16), weights


def from_peers(value):
    ranks = lax.axis_size("dp")
    return [
        lax.ppermute(value, "dp", [(i, (i + k) % ranks) for i in range(ranks)])
        for k in range(1, ranks)
    ]


def body(
    lengths,
    send_slots,
    recv_slots,
    latent_cache,
    queries,
    newest_kv,
    hidden_rows,
    route_ids,
    route_gates,
    w_gate,
    w_up,
    w_down,
):
    slot_count = lengths.shape[0]
    ranks = lax.axis_size("dp")
    rank = lax.axis_index("dp")
    expert = lax.axis_index("ep").astype(jnp.int32)
    expert = jnp.stack([expert, expert + 1 - 2 * (expert % 2)])
    local_slots = jnp.arange(slot_count, dtype=jnp.int32)
    leaving = jnp.min(send_slots)
    vacated = local_slots == leaving
    chosen = jnp.minimum(leaving, slot_count - 1)
    landings = [
        local_slots == lax.dynamic_index_in_dim(recv_slots[0, :, 0], (rank - k) % ranks, 0, False)
        for k in range(1, ranks)
    ]

    rows_one, weights = routed_layer(
        hidden_rows,
        route_columns(route_ids[0, 0], route_gates[0, 0], slot_count),
        expert,
        [w_gate[0], w_up[0], w_down[0]],
    )

    first_att, cache_now = decode_pass(latent_cache, queries[0], newest_kv[0], lengths)
    counts_one = jnp.where(lengths > 0, lengths + 1, 0)
    cache_out = lax.dynamic_index_in_dim(cache_now, chosen, 0, False)
    count_out = lax.dynamic_index_in_dim(counts_one, chosen, 0, True).astype(jnp.bfloat16)
    moving = jnp.concatenate(
        [cache_out, jnp.broadcast_to(count_out, (8, cache_out.shape[1]))], axis=0
    )
    cap = cache_out.shape[0]
    cache_two = cache_now
    counts_two = jnp.where(vacated, 0, counts_one)
    for landing, arrived in zip(landings, from_peers(moving)):
        cache_two = jnp.where(landing[:, None, None], arrived[None, :cap], cache_two)
        counts_two = jnp.where(landing, arrived[cap, 0].astype(jnp.int32), counts_two)
    second_att, unused_cache = decode_pass(cache_two, queries[1], newest_kv[1], counts_two)

    row_out = lax.dynamic_index_in_dim(rows_one, chosen, 0, True)
    rows_two = jnp.where(vacated[:, None], jnp.zeros_like(rows_one), rows_one)
    for landing, row_in in zip(landings, from_peers(row_out)):
        rows_two = jnp.where(landing[:, None], row_in, rows_two)
    final_rows, weights = routed_layer(
        rows_two,
        route_columns(route_ids[1, 0], route_gates[1, 0], slot_count),
        expert,
        weights,
    )
    return (jnp.stack([first_att, second_att]), final_rows)


def solution(mesh):
    return jax.shard_map(
        body,
        mesh=mesh,
        in_specs=(
            P(("dp", "ep")),
            P(("dp", "ep"), None, None),
            P(("dp", "ep"), None, None),
            P(("dp", "ep"), None, None),
            P(None, ("dp", "ep"), None, None),
            P(None, ("dp", "ep"), None),
            P(("dp", "ep"), None),
            P(None, "ep", None, None),
            P(None, "ep", None, None),
            P("ep", None, "dp"),
            P("ep", None, "dp"),
            P("ep", "dp", None),
        ),
        out_specs=(P(None, ("dp", "ep"), None, None), P(("dp", "ep"), None)),
        check_vma=False,
    )
```
